32 devices in a mesh: groups: 2 (over x), seq: 16 (over z, y, core), heads: 1.
Axes of the slice: x: 2, y: 2, z: 4, core: 2. Of those that a mesh axis runs over, the one named last changes fastest.
Arguments:
- x_rows: bfloat16 [10240, 3072], P(('groups', 'seq')), parts along dimension 0, may hold values from -0.125 to 0.125
- queries: bfloat16 [10240, 4096], P(('groups', 'seq'), 'heads'), parts along dimension 0, may hold values from -0.5 to 0.5
- keys: bfloat16 [10240, 4096], P(('groups', 'seq'), 'heads'), parts along dimension 0, may hold values from -0.5 to 0.5
- values: bfloat16 [10240, 4096], P(('groups', 'seq'), 'heads'), parts along dimension 0, may hold values from -0.75 to 0.75
- out_grad: bfloat16 [10240, 4096], P(('groups', 'seq'), 'heads'), parts along dimension 0, may hold values from -0.75 to 0.75
- log_decay: float32 [10240, 32], P(('groups', 'seq'), 'heads'), parts along dimension 0, may hold values from -4 to 0
Outputs:
- query_gradient: bfloat16 [10240, 4096], P(('groups', 'seq'), 'heads'), parts along dimension 0
- key_grad: bfloat16 [10240, 4096], P(('groups', 'seq'), 'heads'), parts along dimension 0
- value_grad: bfloat16 [10240, 4096], P(('groups', 'seq'), 'heads'), parts along dimension 0
- weight_grad: bfloat16 [6144, 4096], P(('groups', 'seq'), 'heads'), parts along dimension 0
The draws below stay inside these ranges and needn't reach their ends.
There are 2 independent parts, one for each index of `groups`. The reference program is written for one: setup_inputs(seed, part) draws one part's arguments, and reference() takes and returns one part's arrays. A program takes and returns all parts, laid end to end along the dimension named above; each array names one. Nothing has to cross between parts.
All inputs are finite; a program needn't handle non-finite values.
Results may differ from the reference program's by a relative error of at most 0.033.
Values may be sent and summed in bfloat16 or wider, within the bound.
A program may use at most 192 MiB of HBM per device.

```python
import math
import jax
import jax.numpy as jnp
from jax import lax

D = 3072
HEADS = 32
HDIM = 128
TOK_DEV = 320
TOKENS = 5120


def draw_log_decay(key, part):
    key = jax.random.fold_in(key, 7)
    keys_list = jax.random.split(key, 7)
    fast_share = 0.5
    blocks = TOKENS // TOK_DEV
    head_pick = jax.random.uniform(keys_list[0], (HEADS,), jnp.float32)
    fast = head_pick < fast_share
    forget_len = jax.random.uniform(keys_list[1], (HEADS,), jnp.float32, 30.0, 50.0)
    fast_rate = math.log(20.0) / forget_len
    slow_rate = 0.35 * jax.random.uniform(keys_list[2], (HEADS,), jnp.float32, 0.3, 1.0) / TOKENS
    base_rate = jnp.where(fast, fast_rate, slow_rate)
    block_mult = jnp.exp(jax.random.uniform(keys_list[3], (blocks, 1, HEADS), jnp.float32, math.log(0.6), math.log(1.5)))
    rough = jax.random.uniform(keys_list[4], (blocks, TOK_DEV, HEADS), jnp.float32, 0.5, 1.5)
    decay_speed = (base_rate[None, None, :] * rough * block_mult).reshape(TOKENS, HEADS)
    token_slots = jax.random.randint(keys_list[5], (2,), 0, TOKENS)
    scan_levels = jnp.log(jax.random.uniform(keys_list[6], (2, HEADS), jnp.float32, 0.5, 0.8))
    token_offsets = jnp.arange(TOKENS)
    token_group_size = jnp.where(token_offsets[:, None] == token_slots[0], scan_levels[0][None, :], 0.0)
    token_group_size = token_group_size + jnp.where(token_offsets[:, None] == token_slots[1], scan_levels[1][None, :], 0.0)
    return (token_group_size - decay_speed).astype(jnp.float32)


def with_spikes(entries, stream_key, source, target, blocks, factor):
    owner, partner = [(jnp.arange(entries.shape[dim]) // (entries.shape[dim] // blocks)).reshape([-1 if axis == dim else 1 for axis in range(entries.ndim)]) for dim in (source, target)]
    chosen = jax.random.permutation(stream_key, blocks)[partner]
    strong = (owner == chosen) | (owner == (partner + blocks // 2) % blocks)
    return jnp.where(strong, factor * entries, entries)


def block_levels(own_key, shape, cuts, low, top_value):
    gain, own = 1.0, jax.random.fold_in(own_key, 6)
    for position, blocks in cuts:
        heights = jnp.exp(jax.random.uniform(jax.random.fold_in(own, position), (blocks,), jnp.float32, low / len(cuts), top_value / len(cuts)))
        gain = gain * jnp.repeat(heights, shape[position] // blocks).reshape([-1 if axis == position else 1 for axis in range(len(shape))])
    return gain


def gaussian(rng, shape, deviation, limit, shards=(), kind=jnp.bfloat16):
    level = block_levels(rng, shape, shards, -0.22, 0.18) if shards else 1.0
    entries = jax.random.normal(rng, shape, jnp.float32) * deviation * level
    return jnp.minimum(jnp.maximum(entries, -limit), limit).astype(kind)


def noise_with(stream_key, extent, scale, most, cuts, heavy, held_as=jnp.bfloat16):
    drawn = scale * jax.random.normal(stream_key, extent, jnp.float32)
    if cuts:
        drawn = drawn * block_levels(stream_key, extent, cuts, -0.22, 0.18)
    return jnp.clip(with_spikes(drawn, jax.random.fold_in(stream_key, 3), *heavy), -most, most).astype(held_as)


def setup_inputs(seed: int = 0, part: int = 0) -> dict:
    splits = jax.random.split(jax.random.key(seed), 7)
    part_splits = jax.random.split(jax.random.fold_in(splits[6], part), 7)
    x_rows = noise_with(part_splits[0], (TOKENS, D), (TOKENS ** -0.5), 0.125, ((0, 16),), (0, 1, 16, 2.0))
    queries = gaussian(part_splits[1], (TOKENS, HEADS * HDIM), (HDIM ** -0.5), 0.5, ((0, 16),))
    keys = gaussian(part_splits[2], (TOKENS, HEADS * HDIM), (HDIM ** -0.5), 0.5, ((0, 16),))
    values = gaussian(part_splits[3], (TOKENS, HEADS * HDIM), (TOKENS ** -0.25), 0.75, ((0, 16),))
    out_grad = gaussian(part_splits[4], (TOKENS, HEADS * HDIM), (TOKENS ** -0.25), 0.75, ((0, 16),))
    log_decay = draw_log_decay(jax.random.fold_in(jax.random.fold_in(splits[6], part), 71), part)
    return dict(x_rows=x_rows, queries=queries, keys=keys, values=values, out_grad=out_grad, log_decay=log_decay)


def block_states(queries, keys, values, output_gradients, cumul):
    span_total = cumul[-1]
    to_end = jnp.exp(span_total[None, :] - cumul)
    since_beginning = jnp.exp(cumul)
    weighted_key_rows = keys.astype(jnp.float32) * to_end[:, :, None]
    key_value_state = jnp.einsum('yzf,yzu->zfu', weighted_key_rows, values.astype(jnp.float32), precision=lax.Precision.HIGHEST)
    scaled_queries = queries.astype(jnp.float32) * since_beginning[:, :, None]
    qd_state = jnp.einsum('thq,thv->hqv', scaled_queries, output_gradients.astype(jnp.float32), precision=lax.Precision.HIGHEST)
    return key_value_state.astype(jnp.bfloat16), qd_state.astype(jnp.bfloat16)


def block_grads(queries, keys, values, output_gradients, cumul, leading_product, suffix):
    length = queries.shape[0]
    span_total = cumul[-1]
    to_end = jnp.exp(span_total[None, :] - cumul)
    since_beginning = jnp.exp(cumul)
    heads_first = cumul.T
    gap_matrix = heads_first[:, :, None] - heads_first[:, None, :]
    steps_row = jnp.arange(length)
    causal = (steps_row[:, None] >= steps_row[None, :])[None]
    decays = jnp.where(causal, jnp.exp(jnp.where(causal, gap_matrix, 0.0)), 0.0)
    query32 = queries.astype(jnp.float32)
    key32 = keys.astype(jnp.float32)
    value32 = values.astype(jnp.float32)
    gradient_single = output_gradients.astype(jnp.float32)
    leading_product_single = leading_product.astype(jnp.float32)
    suffix32 = suffix.astype(jnp.float32)
    upper_precision = lax.Precision.HIGHEST
    scores = jnp.einsum('thv,shv->hts', gradient_single, value32, precision=upper_precision)
    weighted = (scores * decays).astype(jnp.bfloat16).astype(jnp.float32)
    pairs = jnp.einsum('thk,shk->hts', query32, key32, precision=upper_precision)
    mixed = (pairs * decays).astype(jnp.bfloat16).astype(jnp.float32)
    query_gradient = jnp.einsum('hts,shk->thk', weighted, key32, precision=upper_precision)
    query_gradient = query_gradient + since_beginning[:, :, None] * jnp.einsum('znm,nxm->znx', gradient_single, leading_product_single, precision=upper_precision)
    key_grad = jnp.einsum('hts,thk->shk', weighted, query32, precision=upper_precision)
    key_grad = key_grad + to_end[:, :, None] * jnp.einsum('shv,hqv->shq', value32, suffix32, precision=upper_precision)
    value_grad = jnp.einsum('hts,thv->shv', mixed, gradient_single, precision=upper_precision)
    value_grad = value_grad + to_end[:, :, None] * jnp.einsum('shq,hqv->shv', key32, suffix32, precision=upper_precision)
    return query_gradient.astype(jnp.bfloat16), key_grad.astype(jnp.bfloat16), value_grad.astype(jnp.bfloat16)


def reference(x_rows, queries, keys, values, out_grad, log_decay):
    blocks = TOKENS // TOK_DEV
    shaped = (blocks, TOK_DEV, HEADS, HDIM)
    query_heads = queries.reshape(shaped)
    key_heads = keys.reshape(shaped)
    value_heads = values.reshape(shaped)
    grad_heads = out_grad.reshape(shaped)
    cumul = jnp.cumsum(log_decay.reshape(blocks, TOK_DEV, HEADS), axis=1)
    key_value_full, query_decay_full = lax.map(lambda group: block_states(*group), (query_heads, key_heads, value_heads, grad_heads, cumul))
    totals = cumul[:, -1]
    before_sum = jnp.cumsum(totals, axis=0) - totals
    after_sum = before_sum + totals
    rows_i = jnp.arange(blocks)[:, None, None]
    cols_j = jnp.arange(blocks)[None, :, None]
    earlier = cols_j < rows_i
    later = cols_j > rows_i
    preceding_weight = jnp.where(earlier, jnp.exp(jnp.where(earlier, before_sum[:, None, :] - after_sum[None, :, :], 0.0)), 0.0)
    following_weight = jnp.where(later, jnp.exp(jnp.where(later, before_sum[None, :, :] - after_sum[:, None, :], 0.0)), 0.0)
    leading_product = jnp.einsum('ijh,jhkv->ihkv', preceding_weight, key_value_full.astype(jnp.float32), precision=lax.Precision.HIGHEST).astype(jnp.bfloat16)
    suffix = jnp.einsum('ijh,jhkv->ihkv', following_weight, query_decay_full.astype(jnp.float32), precision=lax.Precision.HIGHEST).astype(jnp.bfloat16)
    query_gradient, key_grad, value_grad = lax.map(lambda group: block_grads(*group), (query_heads, key_heads, value_heads, grad_heads, cumul, leading_product, suffix))
    flat = (TOKENS, HEADS * HDIM)
    x_blocks = x_rows.reshape(blocks, TOK_DEV, D)
    value_blocks = value_grad.reshape(blocks, TOK_DEV, HEADS * HDIM)

    def add_block(running, group):
        x_block, value_block = group
        term = jnp.einsum('td,tc->dc', x_block.astype(jnp.float32), value_block.astype(jnp.float32), precision=lax.Precision.HIGHEST)
        rounded = lax.optimization_barrier(term.astype(jnp.bfloat16))
        return running + rounded.astype(jnp.float32), None

    weight_sum, unused = lax.scan(add_block, jnp.zeros((D, HEADS * HDIM), jnp.float32), (x_blocks, value_blocks))
    return query_gradient.reshape(flat), key_grad.reshape(flat), value_grad.reshape(flat), weight_sum.astype(jnp.bfloat16)
```

```python
import functools

import jax
import jax.numpy as jnp
from jax import lax
from jax.experimental import pallas as pl
from jax.experimental.pallas import tpu as pltpu
from jax.sharding import PartitionSpec as P

F32 = jnp.float32
BF16 = jnp.bfloat16
CHUNKS = 4


def dot(a, b, dims):
    return lax.dot_general(a, b, (dims, ((), ())), preferred_element_type=F32)


def columns_of(row, width):
    return jnp.broadcast_to(row, (width, row.shape[1])).T


def decay_matrix(row, width):
    length = row.shape[1]
    gap = columns_of(row, width)[:, :1] - row
    t = lax.broadcasted_iota(jnp.int32, (length, length), 0)
    s = lax.broadcasted_iota(jnp.int32, (length, length), 1)
    return jnp.where(t >= s, jnp.exp(jnp.where(t >= s, gap, 0.0)), 0.0)


def states_kernel(q_ref, k_ref, v_ref, g_ref, cum_ref, kv_ref, qd_ref):
    row = cum_ref[0]
    width = q_ref.shape[1]
    length = row.shape[1]
    cum = columns_of(row, width)
    total = row[:, length - 1 :]
    keys = (k_ref[...].astype(F32) * jnp.exp(total - cum)).astype(BF16)
    queries = (q_ref[...].astype(F32) * jnp.exp(cum)).astype(BF16)
    kv_ref[0] = dot(keys, v_ref[...], ((0,), (0,))).astype(BF16)
    qd_ref[0] = dot(queries, g_ref[...], ((0,), (0,))).astype(BF16)


def value_local_kernel(q_ref, k_ref, g_ref, cum_ref, out_ref):
    decays = decay_matrix(cum_ref[0], q_ref.shape[1])
    mixed = (dot(q_ref[...], k_ref[...], ((1,), (1,))) * decays).astype(BF16)
    out_ref[...] = dot(mixed, g_ref[...], ((0,), (0,)))


def value_finish_kernel(local_ref, k_ref, cum_ref, suffix_ref, out_ref):
    row = cum_ref[0]
    cum = columns_of(row, k_ref.shape[1])
    to_end = jnp.exp(row[:, row.shape[1] - 1 :] - cum)
    part = dot(k_ref[...], suffix_ref[0], ((1,), (0,)))
    out_ref[...] = (local_ref[...] + to_end * part).astype(BF16)


def query_key_kernel(q_ref, k_ref, v_ref, g_ref, cum_ref, prefix_ref, suffix_ref, qg_ref, kg_ref):
    row = cum_ref[0]
    width = q_ref.shape[1]
    cum = columns_of(row, width)
    to_end = jnp.exp(row[:, row.shape[1] - 1 :] - cum)
    decays = decay_matrix(row, width)
    weighted = (dot(g_ref[...], v_ref[...], ((1,), (1,))) * decays).astype(BF16)
    qg = dot(weighted, k_ref[...], ((1,), (0,)))
    qg = qg + jnp.exp(cum) * dot(g_ref[...], prefix_ref[0], ((1,), (1,)))
    kg = dot(weighted, q_ref[...], ((0,), (0,)))
    kg = kg + to_end * dot(v_ref[...], suffix_ref[0], ((1,), (1,)))
    qg_ref[...] = qg.astype(BF16)
    kg_ref[...] = kg.astype(BF16)


def per_head(body, first, count, length, size, kinds, outs, flops, args):
    specs = {
        "w": pl.BlockSpec((length, size), lambda h: (0, first + h)),
        "c": pl.BlockSpec((length, size), lambda h: (0, h)),
        "l": pl.BlockSpec((1, 1, length), lambda h: (first + h, 0, 0)),
        "s": pl.BlockSpec((1, size, size), lambda h: (h, 0, 0)),
    }
    shapes = {
        "c": (length, count * size),
        "s": (count, size, size),
    }
    moved = count * length * size * 2 * (len(kinds) + len(outs))
    return pl.pallas_call(
        body,
        grid=(count,),
        in_specs=[specs[kind] for kind in kinds],
        out_specs=[specs[kind] for kind, _ in outs],
        out_shape=[jax.ShapeDtypeStruct(shapes[kind], dtype) for kind, dtype in outs],
        cost_estimate=pl.CostEstimate(
            flops=count * flops, bytes_accessed=moved, transcendentals=count * length * length
        ),
        compiler_params=pltpu.CompilerParams(vmem_limit_bytes=32 * 1024 * 1024),
    )(*args)


def step(mapping, count):
    return [(i, mapping(i)) for i in range(count) if mapping(i) is not None]


def plane_scan(kv, qd, totals, index):
    heads = kv.shape[0]
    half = heads // 2
    z, y, c = index // 4, (index // 2) % 2, index % 2
    swap_core = step(lambda i: i ^ 1, 16)
    swap_chip = step(lambda i: i ^ 2, 16)
    onward = step(
        lambda i: (i + 4 if i + 4 < 16 else None) if i & 2 else (i - 4 if i >= 4 else None), 16
    )

    def mine(a, which):
        return lax.dynamic_slice_in_dim(a, which * half, half, axis=-3)

    stack = jnp.stack([kv, qd])
    got = lax.ppermute(mine(stack, 1 - c), "seq", swap_core)
    own = mine(stack, c)
    core0 = jnp.where(c == 0, own, got).astype(F32)
    core1 = jnp.where(c == 0, got, own).astype(F32)
    t = lax.dynamic_slice_in_dim(totals, c * half, half, axis=1).reshape(4, 2, 2, half)
    plane_totals = t.sum((1, 2))
    here = lax.dynamic_index_in_dim(t, z, 0, keepdims=False)
    own_chip = lax.dynamic_index_in_dim(here, y, 0, keepdims=False)
    other_chip = lax.dynamic_index_in_dim(here, 1 - y, 0, keepdims=False)

    def scale(log):
        return jnp.exp(log)[:, None, None]

    kv_chip = scale(own_chip[1]) * core0[0] + core1[0]
    qd_chip = core0[1] + scale(own_chip[0]) * core1[1]
    sent = jnp.where(y == 0, kv_chip, qd_chip).astype(BF16)
    neighbour = lax.ppermute(sent, "seq", swap_chip).astype(F32)
    plane = jnp.where(y == 0, qd_chip, kv_chip) + scale(own_chip.sum(0)) * neighbour
    travelling = plane.astype(BF16)
    direction = jnp.where(y == 0, 1, -1)
    beyond = jnp.zeros_like(plane)
    log = jnp.zeros((half,), F32)
    for hop in range(1, 4):
        travelling = lax.ppermute(travelling, "seq", onward)
        beyond = beyond + scale(log) * travelling.astype(F32)
        at = jnp.clip(z + direction * hop, 0, 3)
        log = log + lax.dynamic_index_in_dim(plane_totals, at, 0, keepdims=False)
    beyond = beyond.astype(BF16)
    other = lax.ppermute(beyond, "seq", swap_chip)
    before = jnp.where(y == 1, beyond, other).astype(F32)
    after = jnp.where(y == 0, beyond, other).astype(F32)
    other_scale = scale(other_chip.sum(0))
    before = jnp.where(y == 0, before, other_scale * before + neighbour)
    after = jnp.where(y == 1, after, other_scale * after + neighbour)
    for0 = jnp.stack([before, scale(own_chip[1]) * after + core1[1]])
    for1 = jnp.stack([scale(own_chip[0]) * before + core0[0], after])
    keep = jnp.where(c == 0, for0, for1).astype(BF16)
    give = jnp.where(c == 0, for1, for0).astype(BF16)
    took = lax.ppermute(give, "seq", swap_core)
    low = jnp.where(c == 0, keep, took)
    high = jnp.where(c == 0, took, keep)
    both = jnp.concatenate([low, high], axis=1)
    return both[0], both[1]


def gathered_scan(kv, qd, totals, index):
    kv_all = lax.all_gather(kv[None], "seq", axis=0, tiled=True)
    qd_all = lax.all_gather(qd[None], "seq", axis=0, tiled=True)
    before = jnp.cumsum(totals, axis=0) - totals
    after = before + totals
    own_start = lax.dynamic_index_in_dim(before, index, 0, keepdims=False)
    own_end = lax.dynamic_index_in_dim(after, index, 0, keepdims=False)
    ids = jnp.arange(totals.shape[0])[:, None]
    earlier, later = ids < index, ids > index
    pre = jnp.where(earlier, jnp.exp(jnp.where(earlier, own_start[None] - after, 0.0)), 0.0)
    post = jnp.where(later, jnp.exp(jnp.where(later, before - own_end[None], 0.0)), 0.0)
    prefix = jnp.sum(pre[:, :, None, None] * kv_all.astype(F32), axis=0)
    suffix = jnp.sum(post[:, :, None, None] * qd_all.astype(F32), axis=0)
    return prefix.astype(BF16), suffix.astype(BF16)


def plane_rows(x_rows, index):
    length, width = x_rows.shape
    place = index % 4
    parts = x_rows.reshape(length, 4, 4, width // 16)

    def columns(p):
        return lax.dynamic_index_in_dim(parts, p, 2, keepdims=False).reshape(length, width // 4)

    held = [columns(place)]
    for k in (1, 2, 3):
        held.append(lax.ppermute(columns(place ^ k), "seq", step(lambda i: i ^ k, 16)))
    return jnp.concatenate(held, axis=0).T


def plane_values(dv):
    core = lax.ppermute(dv, "seq", step(lambda i: i ^ 1, 16))
    chip = lax.ppermute(dv, "seq", step(lambda i: i ^ 2, 16))
    both = lax.ppermute(chip, "seq", step(lambda i: i ^ 1, 16))
    return jnp.concatenate([dv, core, chip, both], axis=0)


def planes_sum(blocks, index):
    z = index // 4

    def pick(i):
        return lax.dynamic_index_in_dim(blocks, jnp.clip(i, 0, 3), 0, keepdims=False)

    up = down = None
    for s in (1, 2, 3):
        to_up, to_down = pick(4 - s + z), pick(z - 4 + s)
        if up is not None:
            to_up = (to_up.astype(F32) + up.astype(F32)).astype(BF16)
            to_down = (to_down.astype(F32) + down.astype(F32)).astype(BF16)
        up = lax.ppermute(to_up, "seq", step(lambda i: i + 4 if i // 4 < s else None, 12))
        down = lax.ppermute(
            to_down, "seq", [(15 - a, 15 - b) for a, b in step(lambda i: i + 4 if i // 4 < s else None, 12)]
        )
    return (pick(z).astype(F32) + up.astype(F32) + down.astype(F32)).astype(BF16)


def on_device(blocks, x_rows, queries, keys, values, out_grad, log_decay):
    length, heads = log_decay.shape
    size = queries.shape[1] // heads
    index = lax.axis_index("seq")
    planes = blocks == 16 and x_rows.shape[1] % 16 == 0
    cumul = jnp.cumsum(log_decay, axis=0)
    lines = cumul.T[:, None, :]
    totals = lax.all_gather(cumul[-1:], "seq", axis=0, tiled=True)
    if planes:
        x_held = plane_rows(x_rows, index)
    chunks = CHUNKS if heads % (2 * CHUNKS) == 0 else 1
    count = heads // chunks
    square, state = 2 * length * length * size, 2 * length * size * size
    call = functools.partial(per_head, length=length, size=size)

    states = [
        call(
            states_kernel, i * count, count, kinds="wwwwl", outs=[("s", BF16)] * 2,
            flops=2 * state, args=(queries, keys, values, out_grad, lines),
        )
        for i in range(chunks)
    ]
    local = [
        call(
            value_local_kernel, i * count, count, kinds="wwwl", outs=[("c", F32)],
            flops=2 * square, args=(queries, keys, out_grad, lines),
        )[0]
        for i in range(chunks)
    ]
    scan = plane_scan if planes else gathered_scan
    prefixes, suffixes, value_grads, sums = [], [], [], []
    for i in range(chunks):
        own = slice(i * count, (i + 1) * count)
        prefix, suffix = scan(*states[i], totals[:, own], index)
        prefixes.append(prefix)
        suffixes.append(suffix)
        (dv,) = call(
            value_finish_kernel, i * count, count, kinds="cwls", outs=[("c", BF16)],
            flops=state, args=(local[i], keys, lines, suffix),
        )
        value_grads.append(dv)
        if planes:
            part = dot(x_held, plane_values(dv), ((1,), (0,))).astype(BF16)
            part = part.reshape(4, part.shape[0] // 4, part.shape[1])
            sums.append(planes_sum(part, index))
        else:
            part = dot(x_rows, dv, ((0,), (0,))).astype(BF16)
            sums.append(lax.psum_scatter(part, "seq", scatter_dimension=0, tiled=True))
    query_gradient, key_grad = call(
        query_key_kernel, 0, heads, kinds="wwwwlss", outs=[("c", BF16)] * 2,
        flops=3 * square + 2 * state,
        args=(
            queries, keys, values, out_grad, lines,
            jnp.concatenate(prefixes), jnp.concatenate(suffixes),
        ),
    )
    return (
        query_gradient,
        key_grad,
        jnp.concatenate(value_grads, axis=1),
        jnp.concatenate(sums, axis=1),
    )


def solution(mesh):
    spread = P(("groups", "seq"), "heads")
    return jax.shard_map(
        functools.partial(on_device, mesh.shape["seq"]),
        mesh=mesh,
        in_specs=(P(("groups", "seq"), None),) + (spread,) * 5,
        out_specs=(spread,) * 4,
        check_vma=False,
    )
```

```python
import functools

import jax
import jax.numpy as jnp
from jax import lax
from jax.experimental import pallas as pl
from jax.experimental.pallas import tpu as pltpu
from jax.sharding import PartitionSpec as P

F32 = jnp.float32
BF16 = jnp.bfloat16
CHUNKS = 4


def dot(a, b, dims):
    return lax.dot_general(a, b, (dims, ((), ())), preferred_element_type=F32)


def columns_of(row, width):
    return jnp.broadcast_to(row, (width, row.shape[1])).T


def decay_matrix(row, width):
    length = row.shape[1]
    gap = columns_of(row, width)[:, :1] - row
    t = lax.broadcasted_iota(jnp.int32, (length, length), 0)
    s = lax.broadcasted_iota(jnp.int32, (length, length), 1)
    return jnp.where(t >= s, jnp.exp(jnp.where(t >= s, gap, 0.0)), 0.0)


def states_kernel(q_ref, k_ref, v_ref, g_ref, cum_ref, kv_ref, qd_ref):
    row = cum_ref[0]
    width = q_ref.shape[1]
    length = row.shape[1]
    cum = columns_of(row, width)
    total = row[:, length - 1 :]
    keys = (k_ref[...].astype(F32) * jnp.exp(total - cum)).astype(BF16)
    queries = (q_ref[...].astype(F32) * jnp.exp(cum)).astype(BF16)
    kv_ref[0] = dot(keys, v_ref[...], ((0,), (0,))).astype(BF16)
    qd_ref[0] = dot(queries, g_ref[...], ((0,), (0,))).astype(BF16)


def value_local_kernel(q_ref, k_ref, g_ref, cum_ref, out_ref):
    decays = decay_matrix(cum_ref[0], q_ref.shape[1])
    mixed = (dot(q_ref[...], k_ref[...], ((1,), (1,))) * decays).astype(BF16)
    out_ref[...] = dot(mixed, g_ref[...], ((0,), (0,)))


def value_finish_kernel(local_ref, k_ref, cum_ref, suffix_ref, out_ref):
    row = cum_ref[0]
    cum = columns_of(row, k_ref.shape[1])
    to_end = jnp.exp(row[:, row.shape[1] - 1 :] - cum)
    part = dot(k_ref[...], suffix_ref[0], ((1,), (0,)))
    out_ref[...] = (local_ref[...] + to_end * part).astype(BF16)


def query_key_kernel(q_ref, k_ref, v_ref, g_ref, cum_ref, prefix_ref, suffix_ref, qg_ref, kg_ref):
    row = cum_ref[0]
    width = q_ref.shape[1]
    cum = columns_of(row, width)
    to_end = jnp.exp(row[:, row.shape[1] - 1 :] - cum)
    decays = decay_matrix(row, width)
    weighted = (dot(g_ref[...], v_ref[...], ((1,), (1,))) * decays).astype(BF16)
    qg = dot(weighted, k_ref[...], ((1,), (0,)))
    qg = qg + jnp.exp(cum) * dot(g_ref[...], prefix_ref[0], ((1,), (1,)))
    kg = dot(weighted, q_ref[...], ((0,), (0,)))
    kg = kg + to_end * dot(v_ref[...], suffix_ref[0], ((1,), (1,)))
    qg_ref[...] = qg.astype(BF16)
    kg_ref[...] = kg.astype(BF16)


def per_head(body, first, count, length, size, kinds, outs, flops, args):
    specs = {
        "w": pl.BlockSpec((length, size), lambda h: (0, first + h)),
        "c": pl.BlockSpec((length, size), lambda h: (0, h)),
        "l": pl.BlockSpec((1, 1, length), lambda h: (first + h, 0, 0)),
        "s": pl.BlockSpec((1, size, size), lambda h: (h, 0, 0)),
    }
    shapes = {
        "c": (length, count * size),
        "s": (count, size, size),
    }
    moved = count * length * size * 2 * (len(kinds) + len(outs))
    return pl.pallas_call(
        body,
        grid=(count,),
        in_specs=[specs[kind] for kind in kinds],
        out_specs=[specs[kind] for kind, _ in outs],
        out_shape=[jax.ShapeDtypeStruct(shapes[kind], dtype) for kind, dtype in outs],
        cost_estimate=pl.CostEstimate(
            flops=count * flops, bytes_accessed=moved, transcendentals=count * length * length
        ),
        compiler_params=pltpu.CompilerParams(vmem_limit_bytes=32 * 1024 * 1024),
    )(*args)


def mega_kernel(
    blocks, x_ref, q_ref, k_ref, v_ref, g_ref, cum_ref, prefix_ref, suffix_ref,
    qg_ref, kg_ref, dv_ref, wg_ref,
    held, part, landed, plane_send, plane_recv, line_send, line_recv,
):
    index = lax.axis_index("seq")
    z = index // 4
    last = blocks // 4 - 1
    core, chip = index + 1 - 2 * (index % 2), index + 2 - 4 * ((index // 2) % 2)
    chunks, length, width = held.shape[0], q_ref.shape[0], held.shape[2]
    size = prefix_ref.shape[1]
    group = width // size
    rows = part.shape[2]

    barrier = pltpu.get_barrier_semaphore()

    def greet(device):
        pl.semaphore_signal(
            barrier, inc=1, device_id={"seq": device}, device_id_type=pl.DeviceIdType.MESH
        )

    greet(core)
    greet(chip)

    @pl.when(z > 0)
    def _():
        greet(index - 4)

    @pl.when(z < last)
    def _():
        greet(index + 4)

    inner = (z > 0) & (z < last)
    pl.when(inner)(lambda: pl.semaphore_wait(barrier, 4))
    pl.when(jnp.logical_not(inner))(lambda: pl.semaphore_wait(barrier, 3))

    def plane_copy(j, source, target, device):
        return pltpu.make_async_remote_copy(
            src_ref=held.at[j, pl.ds(source * length, length)],
            dst_ref=held.at[j, pl.ds(target * length, length)],
            send_sem=plane_send.at[target - 1, j],
            recv_sem=plane_recv.at[target - 1, j],
            device_id={"seq": device},
            device_id_type=pl.DeviceIdType.MESH,
        )

    def to_core(j):
        return plane_copy(j, 0, 1, core)

    def to_chip(j):
        return plane_copy(j, 0, 2, chip)

    def onward(j):
        return plane_copy(j, 2, 3, core)

    def line_copy(j, way, t):
        slot = t - 1 + way
        return pltpu.make_async_remote_copy(
            src_ref=part.at[j, t],
            dst_ref=landed.at[way, slot, j],
            send_sem=line_send.at[way, slot, j],
            recv_sem=line_recv.at[way, slot, j],
            device_id={"seq": index + 4 - 8 * way},
            device_id_type=pl.DeviceIdType.MESH,
        )

    def columns(j, h):
        return pl.ds(pl.multiple_of(j * width + h * size, size), size)

    def value_part(j):
        for h in range(group):
            at = columns(j, h)
            row = cum_ref[j * group + h]
            cum = columns_of(row, size)
            to_end = jnp.exp(row[:, length - 1 :] - cum)
            keys, grads = k_ref[:, at], g_ref[:, at]
            mixed = (dot(q_ref[:, at], keys, ((1,), (1,))) * decay_matrix(row, size)).astype(BF16)
            dv = dot(mixed, grads, ((0,), (0,)))
            dv = dv + to_end * dot(keys, suffix_ref[j * group + h], ((1,), (0,)))
            dv = dv.astype(BF16)
            dv_ref[:, at] = dv
            held[j, pl.ds(0, length), h * size : (h + 1) * size] = dv

    def query_key_part(j):
        for h in range(group):
            at = columns(j, h)
            row = cum_ref[j * group + h]
            cum = columns_of(row, size)
            to_end = jnp.exp(row[:, length - 1 :] - cum)
            keys, grads, values, queries = k_ref[:, at], g_ref[:, at], v_ref[:, at], q_ref[:, at]
            weighted = dot(grads, values, ((1,), (1,))) * decay_matrix(row, size)
            weighted = weighted.astype(BF16)
            qg = dot(weighted, keys, ((1,), (0,)))
            qg = qg + jnp.exp(cum) * dot(grads, prefix_ref[j * group + h], ((1,), (1,)))
            kg = dot(weighted, queries, ((0,), (0,)))
            kg = kg + to_end * dot(values, suffix_ref[j * group + h], ((1,), (1,)))
            qg_ref[:, at] = qg.astype(BF16)
            kg_ref[:, at] = kg.astype(BF16)

    def within(j):
        return (j >= 0) & (j < chunks)

    def line_part(j, way, t):
        has_source = z > 0 if way == 0 else z < last
        ahead = t > z if way == 0 else t < z

        @pl.when(has_source)
        def _():
            line_copy(j, way, t).wait_recv()
            slot = t - 1 + way
            part[j, t] = (part[j, t].astype(F32) + landed[way, slot, j].astype(F32)).astype(BF16)

        @pl.when(ahead)
        def _():
            line_copy(j, way, t).start()

    def line_stage(j, way):
        order = range(last, 0, -1) if way == 0 else range(last)
        for t in order:
            reached = z <= t if way == 0 else z >= t
            pl.when(within(j) & reached)(functools.partial(line_part, j, way, t))

    @pl.loop(0, chunks + 2 + last)
    def _(i):
        @pl.when(i < chunks)
        def _():
            value_part(i)
            to_chip(i).start()
            to_core(i).start()

        @pl.when(within(i - 1))
        def _():
            to_chip(i - 1).wait_recv()
            onward(i - 1).start()

        j = i - 2

        @pl.when(within(j))
        def _():
            to_core(j).wait_recv()
            onward(j).wait_recv()
            for t in range(last + 1):
                part[j, t] = dot(
                    x_ref[t * rows : (t + 1) * rows, :], held[j], ((1,), (0,))
                ).astype(BF16)

        line_stage(j - z, 0)
        line_stage(j - last + z, 1)

        @pl.when(within(j))
        def _():
            query_key_part(j)

        done = j - last

        @pl.when(within(done))
        def _():
            at = pl.ds(pl.multiple_of(done * width, width), width)
            wg_ref[:, at] = part[done, z]

    @pl.loop(0, chunks)
    def _(j):
        to_core(j).wait_send()
        to_chip(j).wait_send()
        onward(j).wait_send()
        for t in range(last + 1):
            if t > 0:
                pl.when(t > z)(lambda t=t: line_copy(j, 0, t).wait_send())
            if t < last:
                pl.when(t < z)(lambda t=t: line_copy(j, 1, t).wait_send())


def mega(blocks, chunks, x_held, queries, keys, values, out_grad, lines, prefix, suffix):
    length, columns = queries.shape
    width, planes = columns // chunks, blocks // 4
    rows = x_held.shape[0] // planes
    heads, size = prefix.shape[0], prefix.shape[1]
    vmem = pl.BlockSpec(memory_space=pltpu.VMEM)
    whole = jax.ShapeDtypeStruct((length, columns), BF16)
    dma = pltpu.SemaphoreType.DMA
    return pl.pallas_call(
        functools.partial(mega_kernel, blocks),
        out_shape=[whole, whole, whole, jax.ShapeDtypeStruct((rows, columns), BF16)],
        in_specs=[vmem] * 8,
        out_specs=[vmem] * 4,
        scratch_shapes=[
            pltpu.VMEM((chunks, 4 * length, width), BF16),
            pltpu.VMEM((chunks, planes, rows, width), BF16),
            pltpu.VMEM((2, planes - 1, chunks, rows, width), BF16),
            dma((3, chunks)),
            dma((3, chunks)),
            dma((2, planes - 1, chunks)),
            dma((2, planes - 1, chunks)),
        ],
        cost_estimate=pl.CostEstimate(
            flops=heads * (10 * length * length * size + 8 * length * size * size)
            + 2 * x_held.size * columns * 4,
            bytes_accessed=16 * length * columns,
            transcendentals=2 * heads * length * length,
        ),
        compiler_params=pltpu.CompilerParams(
            collective_id=0, has_side_effects=True, vmem_limit_bytes=60 * 1024 * 1024
        ),
    )(x_held, queries, keys, values, out_grad, lines, prefix, suffix)


def step(mapping, count):
    return [(i, mapping(i)) for i in range(count) if mapping(i) is not None]


def plane_scan(kv, qd, totals, index):
    heads = kv.shape[0]
    half = heads // 2
    z, y, c = index // 4, (index // 2) % 2, index % 2
    swap_core = step(lambda i: i ^ 1, 16)
    swap_chip = step(lambda i: i ^ 2, 16)
    onward = step(
        lambda i: (i + 4 if i + 4 < 16 else None) if i & 2 else (i - 4 if i >= 4 else None), 16
    )

    def mine(a, which):
        return lax.dynamic_slice_in_dim(a, which * half, half, axis=-3)

    stack = jnp.stack([kv, qd])
    got = lax.ppermute(mine(stack, 1 - c), "seq", swap_core)
    own = mine(stack, c)
    core0 = jnp.where(c == 0, own, got).astype(F32)
    core1 = jnp.where(c == 0, got, own).astype(F32)
    t = lax.dynamic_slice_in_dim(totals, c * half, half, axis=1).reshape(4, 2, 2, half)
    plane_totals = t.sum((1, 2))
    here = lax.dynamic_index_in_dim(t, z, 0, keepdims=False)
    own_chip = lax.dynamic_index_in_dim(here, y, 0, keepdims=False)
    other_chip = lax.dynamic_index_in_dim(here, 1 - y, 0, keepdims=False)

    def scale(log):
        return jnp.exp(log)[:, None, None]

    kv_chip = scale(own_chip[1]) * core0[0] + core1[0]
    qd_chip = core0[1] + scale(own_chip[0]) * core1[1]
    sent = jnp.where(y == 0, kv_chip, qd_chip).astype(BF16)
    neighbour = lax.ppermute(sent, "seq", swap_chip).astype(F32)
    plane = jnp.where(y == 0, qd_chip, kv_chip) + scale(own_chip.sum(0)) * neighbour
    travelling = plane.astype(BF16)
    direction = jnp.where(y == 0, 1, -1)
    beyond = jnp.zeros_like(plane)
    log = jnp.zeros((half,), F32)
    for hop in range(1, 4):
        travelling = lax.ppermute(travelling, "seq", onward)
        beyond = beyond + scale(log) * travelling.astype(F32)
        at = jnp.clip(z + direction * hop, 0, 3)
        log = log + lax.dynamic_index_in_dim(plane_totals, at, 0, keepdims=False)
    beyond = beyond.astype(BF16)
    other = lax.ppermute(beyond, "seq", swap_chip)
    before = jnp.where(y == 1, beyond, other).astype(F32)
    after = jnp.where(y == 0, beyond, other).astype(F32)
    other_scale = scale(other_chip.sum(0))
    before = jnp.where(y == 0, before, other_scale * before + neighbour)
    after = jnp.where(y == 1, after, other_scale * after + neighbour)
    for0 = jnp.stack([before, scale(own_chip[1]) * after + core1[1]])
    for1 = jnp.stack([scale(own_chip[0]) * before + core0[0], after])
    keep = jnp.where(c == 0, for0, for1).astype(BF16)
    give = jnp.where(c == 0, for1, for0).astype(BF16)
    took = lax.ppermute(give, "seq", swap_core)
    low = jnp.where(c == 0, keep, took)
    high = jnp.where(c == 0, took, keep)
    both = jnp.concatenate([low, high], axis=1)
    return both[0], both[1]


def gathered_scan(kv, qd, totals, index):
    kv_all = lax.all_gather(kv[None], "seq", axis=0, tiled=True)
    qd_all = lax.all_gather(qd[None], "seq", axis=0, tiled=True)
    before = jnp.cumsum(totals, axis=0) - totals
    after = before + totals
    own_start = lax.dynamic_index_in_dim(before, index, 0, keepdims=False)
    own_end = lax.dynamic_index_in_dim(after, index, 0, keepdims=False)
    ids = jnp.arange(totals.shape[0])[:, None]
    earlier, later = ids < index, ids > index
    pre = jnp.where(earlier, jnp.exp(jnp.where(earlier, own_start[None] - after, 0.0)), 0.0)
    post = jnp.where(later, jnp.exp(jnp.where(later, before - own_end[None], 0.0)), 0.0)
    prefix = jnp.sum(pre[:, :, None, None] * kv_all.astype(F32), axis=0)
    suffix = jnp.sum(post[:, :, None, None] * qd_all.astype(F32), axis=0)
    return prefix.astype(BF16), suffix.astype(BF16)


def plane_rows(x_rows, index):
    length, width = x_rows.shape
    place = index % 4
    parts = x_rows.reshape(length, 4, 4, width // 16)

    def columns(p):
        return lax.dynamic_index_in_dim(parts, p, 2, keepdims=False).reshape(length, width // 4)

    held = [columns(place)]
    for k in (1, 2, 3):
        held.append(lax.ppermute(columns(place ^ k), "seq", step(lambda i: i ^ k, 16)))
    return jnp.concatenate(held, axis=0).T


def plane_values(dv):
    core = lax.ppermute(dv, "seq", step(lambda i: i ^ 1, 16))
    chip = lax.ppermute(dv, "seq", step(lambda i: i ^ 2, 16))
    both = lax.ppermute(chip, "seq", step(lambda i: i ^ 1, 16))
    return jnp.concatenate([dv, core, chip, both], axis=0)


def planes_sum(blocks, index):
    z = index // 4

    def pick(i):
        return lax.dynamic_index_in_dim(blocks, jnp.clip(i, 0, 3), 0, keepdims=False)

    up = down = None
    for s in (1, 2, 3):
        to_up, to_down = pick(4 - s + z), pick(z - 4 + s)
        if up is not None:
            to_up = (to_up.astype(F32) + up.astype(F32)).astype(BF16)
            to_down = (to_down.astype(F32) + down.astype(F32)).astype(BF16)
        up = lax.ppermute(to_up, "seq", step(lambda i: i + 4 if i // 4 < s else None, 12))
        down = lax.ppermute(
            to_down, "seq", [(15 - a, 15 - b) for a, b in step(lambda i: i + 4 if i // 4 < s else None, 12)]
        )
    return (pick(z).astype(F32) + up.astype(F32) + down.astype(F32)).astype(BF16)


def on_device(blocks, x_rows, queries, keys, values, out_grad, log_decay):
    length, heads = log_decay.shape
    size = queries.shape[1] // heads
    index = lax.axis_index("seq")
    planes = blocks == 16 and x_rows.shape[1] % 16 == 0
    cumul = jnp.cumsum(log_decay, axis=0)
    lines = cumul.T[:, None, :]
    totals = lax.all_gather(cumul[-1:], "seq", axis=0, tiled=True)
    if planes:
        x_held = plane_rows(x_rows, index)
    chunks = CHUNKS if heads % (2 * CHUNKS) == 0 else 1
    count = heads // chunks
    square, state = 2 * length * length * size, 2 * length * size * size
    call = functools.partial(per_head, length=length, size=size)

    if planes and heads % 8 == 0:
        kv, qd = call(
            states_kernel, 0, heads, kinds="wwwwl", outs=[("s", BF16)] * 2,
            flops=2 * state, args=(queries, keys, values, out_grad, lines),
        )
        prefix, suffix = plane_scan(kv, qd, totals, index)
        return mega(
            blocks, 8, x_held, queries, keys, values, out_grad, lines, prefix, suffix
        )

    states = [
        call(
            states_kernel, i * count, count, kinds="wwwwl", outs=[("s", BF16)] * 2,
            flops=2 * state, args=(queries, keys, values, out_grad, lines),
        )
        for i in range(chunks)
    ]
    local = [
        call(
            value_local_kernel, i * count, count, kinds="wwwl", outs=[("c", F32)],
            flops=2 * square, args=(queries, keys, out_grad, lines),
        )[0]
        for i in range(chunks)
    ]
    scan = plane_scan if planes else gathered_scan
    prefixes, suffixes, value_grads, sums = [], [], [], []
    for i in range(chunks):
        own = slice(i * count, (i + 1) * count)
        prefix, suffix = scan(*states[i], totals[:, own], index)
        prefixes.append(prefix)
        suffixes.append(suffix)
        (dv,) = call(
            value_finish_kernel, i * count, count, kinds="cwls", outs=[("c", BF16)],
            flops=state, args=(local[i], keys, lines, suffix),
        )
        value_grads.append(dv)
        if planes:
            part = dot(x_held, plane_values(dv), ((1,), (0,))).astype(BF16)
            part = part.reshape(4, part.shape[0] // 4, part.shape[1])
            sums.append(planes_sum(part, index))
        else:
            part = dot(x_rows, dv, ((0,), (0,))).astype(BF16)
            sums.append(lax.psum_scatter(part, "seq", scatter_dimension=0, tiled=True))
    query_gradient, key_grad = call(
        query_key_kernel, 0, heads, kinds="wwwwlss", outs=[("c", BF16)] * 2,
        flops=3 * square + 2 * state,
        args=(
            queries, keys, values, out_grad, lines,
            jnp.concatenate(prefixes), jnp.concatenate(suffixes),
        ),
    )
    return (
        query_gradient,
        key_grad,
        jnp.concatenate(value_grads, axis=1),
        jnp.concatenate(sums, axis=1),
    )


def solution(mesh):
    spread = P(("groups", "seq"), "heads")
    return jax.shard_map(
        functools.partial(on_device, mesh.shape["seq"]),
        mesh=mesh,
        in_specs=(P(("groups", "seq"), None),) + (spread,) * 5,
        out_specs=(spread,) * 4,
        check_vma=False,
    )
```

```python
import functools

import jax
import jax.numpy as jnp
from jax import lax
from jax.experimental import pallas as pl
from jax.experimental.pallas import tpu as pltpu
from jax.sharding import PartitionSpec as P

F32 = jnp.float32
BF16 = jnp.bfloat16
CHUNKS = 4


def dot(a, b, dims):
    return lax.dot_general(a, b, (dims, ((), ())), preferred_element_type=F32)


def columns_of(row, width):
    return jnp.broadcast_to(row, (width, row.shape[1])).T


def decay_matrix(row, width):
    length = row.shape[1]
    gap = columns_of(row, width)[:, :1] - row
    t = lax.broadcasted_iota(jnp.int32, (length, length), 0)
    s = lax.broadcasted_iota(jnp.int32, (length, length), 1)
    return jnp.where(t >= s, jnp.exp(jnp.where(t >= s, gap, 0.0)), 0.0)


def states_kernel(q_ref, k_ref, v_ref, g_ref, cum_ref, kv_ref, qd_ref):
    row = cum_ref[0]
    width = q_ref.shape[1]
    length = row.shape[1]
    cum = columns_of(row, width)
    total = row[:, length - 1 :]
    keys = (k_ref[...].astype(F32) * jnp.exp(total - cum)).astype(BF16)
    queries = (q_ref[...].astype(F32) * jnp.exp(cum)).astype(BF16)
    kv_ref[0] = dot(keys, v_ref[...], ((0,), (0,))).astype(BF16)
    qd_ref[0] = dot(queries, g_ref[...], ((0,), (0,))).astype(BF16)


def value_local_kernel(q_ref, k_ref, g_ref, cum_ref, out_ref):
    decays = decay_matrix(cum_ref[0], q_ref.shape[1])
    mixed = (dot(q_ref[...], k_ref[...], ((1,), (1,))) * decays).astype(BF16)
    out_ref[...] = dot(mixed, g_ref[...], ((0,), (0,)))


def value_finish_kernel(local_ref, k_ref, cum_ref, suffix_ref, out_ref):
    row = cum_ref[0]
    cum = columns_of(row, k_ref.shape[1])
    to_end = jnp.exp(row[:, row.shape[1] - 1 :] - cum)
    part = dot(k_ref[...], suffix_ref[0], ((1,), (0,)))
    out_ref[...] = (local_ref[...] + to_end * part).astype(BF16)


def query_key_kernel(q_ref, k_ref, v_ref, g_ref, cum_ref, prefix_ref, suffix_ref, qg_ref, kg_ref):
    row = cum_ref[0]
    width = q_ref.shape[1]
    cum = columns_of(row, width)
    to_end = jnp.exp(row[:, row.shape[1] - 1 :] - cum)
    decays = decay_matrix(row, width)
    weighted = (dot(g_ref[...], v_ref[...], ((1,), (1,))) * decays).astype(BF16)
    qg = dot(weighted, k_ref[...], ((1,), (0,)))
    qg = qg + jnp.exp(cum) * dot(g_ref[...], prefix_ref[0], ((1,), (1,)))
    kg = dot(weighted, q_ref[...], ((0,), (0,)))
    kg = kg + to_end * dot(v_ref[...], suffix_ref[0], ((1,), (1,)))
    qg_ref[...] = qg.astype(BF16)
    kg_ref[...] = kg.astype(BF16)


def per_head(body, first, count, length, size, kinds, outs, flops, args):
    specs = {
        "w": pl.BlockSpec((length, size), lambda h: (0, first + h)),
        "c": pl.BlockSpec((length, size), lambda h: (0, h)),
        "l": pl.BlockSpec((1, 1, length), lambda h: (first + h, 0, 0)),
        "s": pl.BlockSpec((1, size, size), lambda h: (h, 0, 0)),
    }
    shapes = {
        "c": (length, count * size),
        "s": (count, size, size),
    }
    moved = count * length * size * 2 * (len(kinds) + len(outs))
    return pl.pallas_call(
        body,
        grid=(count,),
        in_specs=[specs[kind] for kind in kinds],
        out_specs=[specs[kind] for kind, _ in outs],
        out_shape=[jax.ShapeDtypeStruct(shapes[kind], dtype) for kind, dtype in outs],
        cost_estimate=pl.CostEstimate(
            flops=count * flops, bytes_accessed=moved, transcendentals=count * length * length
        ),
        compiler_params=pltpu.CompilerParams(vmem_limit_bytes=32 * 1024 * 1024),
    )(*args)


def mega_kernel(
    blocks, x_ref, q_ref, k_ref, v_ref, g_ref, cum_ref, prefix_ref, suffix_ref,
    qg_ref, kg_ref, dv_ref, wg_ref,
    held, part, landed, plane_send, plane_recv, line_send, line_recv,
):
    index = lax.axis_index("seq")
    z = index // 4
    last = blocks // 4 - 1
    core, chip = index + 1 - 2 * (index % 2), index + 2 - 4 * ((index // 2) % 2)
    chunks, length, width = held.shape[0], q_ref.shape[0], held.shape[2]
    size = prefix_ref.shape[1]
    group = width // size
    rows = part.shape[2]

    barrier = pltpu.get_barrier_semaphore()

    def greet(device):
        pl.semaphore_signal(
            barrier, inc=1, device_id={"seq": device}, device_id_type=pl.DeviceIdType.MESH
        )

    greet(core)
    greet(chip)

    @pl.when(z > 0)
    def _():
        greet(index - 4)

    @pl.when(z < last)
    def _():
        greet(index + 4)

    inner = (z > 0) & (z < last)
    pl.when(inner)(lambda: pl.semaphore_wait(barrier, 4))
    pl.when(jnp.logical_not(inner))(lambda: pl.semaphore_wait(barrier, 3))

    def plane_copy(j, source, target, device):
        return pltpu.make_async_remote_copy(
            src_ref=held.at[j, pl.ds(source * length, length)],
            dst_ref=held.at[j, pl.ds(target * length, length)],
            send_sem=plane_send.at[target - 1, j],
            recv_sem=plane_recv.at[target - 1, j],
            device_id={"seq": device},
            device_id_type=pl.DeviceIdType.MESH,
        )

    def to_core(j):
        return plane_copy(j, 0, 1, core)

    def to_chip(j):
        return plane_copy(j, 0, 2, chip)

    def onward(j):
        return plane_copy(j, 2, 3, core)

    def line_copy(j, way, t):
        slot = t - 1 + way
        return pltpu.make_async_remote_copy(
            src_ref=part.at[j, t],
            dst_ref=landed.at[way, slot, j],
            send_sem=line_send.at[way, slot, j],
            recv_sem=line_recv.at[way, slot, j],
            device_id={"seq": index + 4 - 8 * way},
            device_id_type=pl.DeviceIdType.MESH,
        )

    def columns(j, h):
        return pl.ds(pl.multiple_of(j * width + h * size, size), size)

    def value_part(j):
        for h in range(group):
            at = columns(j, h)
            row = cum_ref[j * group + h]
            cum = columns_of(row, size)
            to_end = jnp.exp(row[:, length - 1 :] - cum)
            keys, grads = k_ref[:, at], g_ref[:, at]
            mixed = (dot(q_ref[:, at], keys, ((1,), (1,))) * decay_matrix(row, size)).astype(BF16)
            dv = dot(mixed, grads, ((0,), (0,)))
            dv = dv + to_end * dot(keys, suffix_ref[j * group + h], ((1,), (0,)))
            dv = dv.astype(BF16)
            dv_ref[:, at] = dv
            held[j, pl.ds(0, length), h * size : (h + 1) * size] = dv

    def query_key_part(j):
        for h in range(group):
            at = columns(j, h)
            row = cum_ref[j * group + h]
            cum = columns_of(row, size)
            to_end = jnp.exp(row[:, length - 1 :] - cum)
            keys, grads, values, queries = k_ref[:, at], g_ref[:, at], v_ref[:, at], q_ref[:, at]
            weighted = dot(grads, values, ((1,), (1,))) * decay_matrix(row, size)
            weighted = weighted.astype(BF16)
            qg = dot(weighted, keys, ((1,), (0,)))
            qg = qg + jnp.exp(cum) * dot(grads, prefix_ref[j * group + h], ((1,), (1,)))
            kg = dot(weighted, queries, ((0,), (0,)))
            kg = kg + to_end * dot(values, suffix_ref[j * group + h], ((1,), (1,)))
            qg_ref[:, at] = qg.astype(BF16)
            kg_ref[:, at] = kg.astype(BF16)

    def within(j):
        return (j >= 0) & (j < chunks)

    def line_part(j, way, t):
        has_source = z > 0 if way == 0 else z < last
        ahead = t > z if way == 0 else t < z

        @pl.when(has_source)
        def _():
            line_copy(j, way, t).wait_recv()
            slot = t - 1 + way
            part[j, t] = (part[j, t].astype(F32) + landed[way, slot, j].astype(F32)).astype(BF16)

        @pl.when(ahead)
        def _():
            line_copy(j, way, t).start()

    def line_stage(j, way):
        order = range(last, 0, -1) if way == 0 else range(last)
        for t in order:
            reached = z <= t if way == 0 else z >= t
            pl.when(within(j) & reached)(functools.partial(line_part, j, way, t))

    @pl.loop(0, chunks + 2 + last)
    def _(i):
        @pl.when(i < chunks)
        def _():
            value_part(i)
            to_chip(i).start()
            to_core(i).start()

        @pl.when(within(i - 1))
        def _():
            to_chip(i - 1).wait_recv()
            onward(i - 1).start()

        j = i - 2

        @pl.when(within(j))
        def _():
            to_core(j).wait_recv()
            onward(j).wait_recv()
            for t in range(last + 1):
                part[j, t] = dot(
                    x_ref[t * rows : (t + 1) * rows, :], held[j], ((1,), (0,))
                ).astype(BF16)

        line_stage(j - z, 0)
        line_stage(j - last + z, 1)

        @pl.when(within(j))
        def _():
            query_key_part(j)

        done = j - last

        @pl.when(within(done))
        def _():
            at = pl.ds(pl.multiple_of(done * width, width), width)
            wg_ref[:, at] = part[done, z]

    @pl.loop(0, chunks)
    def _(j):
        to_core(j).wait_send()
        to_chip(j).wait_send()
        onward(j).wait_send()
        for t in range(last + 1):
            if t > 0:
                pl.when(t > z)(lambda t=t: line_copy(j, 0, t).wait_send())
            if t < last:
                pl.when(t < z)(lambda t=t: line_copy(j, 1, t).wait_send())


def mega(blocks, chunks, x_held, queries, keys, values, out_grad, lines, prefix, suffix):
    length, columns = queries.shape
    width, planes = columns // chunks, blocks // 4
    rows = x_held.shape[0] // planes
    heads, size = prefix.shape[0], prefix.shape[1]
    vmem = pl.BlockSpec(memory_space=pltpu.VMEM)
    whole = jax.ShapeDtypeStruct((length, columns), BF16)
    dma = pltpu.SemaphoreType.DMA
    return pl.pallas_call(
        functools.partial(mega_kernel, blocks),
        out_shape=[whole, whole, whole, jax.ShapeDtypeStruct((rows, columns), BF16)],
        in_specs=[vmem] * 8,
        out_specs=[vmem] * 4,
        scratch_shapes=[
            pltpu.VMEM((chunks, 4 * length, width), BF16),
            pltpu.VMEM((chunks, planes, rows, width), BF16),
            pltpu.VMEM((2, planes - 1, chunks, rows, width), BF16),
            dma((3, chunks)),
            dma((3, chunks)),
            dma((2, planes - 1, chunks)),
            dma((2, planes - 1, chunks)),
        ],
        cost_estimate=pl.CostEstimate(
            flops=heads * (10 * length * length * size + 8 * length * size * size)
            + 2 * x_held.size * columns * 4,
            bytes_accessed=16 * length * columns,
            transcendentals=2 * heads * length * length,
        ),
        compiler_params=pltpu.CompilerParams(
            collective_id=0, has_side_effects=True, vmem_limit_bytes=60 * 1024 * 1024
        ),
    )(x_held, queries, keys, values, out_grad, lines, prefix, suffix)


def step(mapping, count):
    return [(i, mapping(i)) for i in range(count) if mapping(i) is not None]


def plane_scan(kv, qd, totals, index):
    heads = kv.shape[0]
    half = heads // 2
    z, y, c = index // 4, (index // 2) % 2, index % 2
    swap_core = step(lambda i: i ^ 1, 16)
    swap_chip = step(lambda i: i ^ 2, 16)
    onward = step(
        lambda i: (i + 4 if i + 4 < 16 else None) if i & 2 else (i - 4 if i >= 4 else None), 16
    )

    def mine(a, which):
        return lax.dynamic_slice_in_dim(a, which * half, half, axis=-3)

    stack = jnp.stack([kv, qd])
    got = lax.ppermute(mine(stack, 1 - c), "seq", swap_core)
    own = mine(stack, c)
    core0 = jnp.where(c == 0, own, got).astype(F32)
    core1 = jnp.where(c == 0, got, own).astype(F32)
    t = lax.dynamic_slice_in_dim(totals, c * half, half, axis=1).reshape(4, 2, 2, half)
    plane_totals = t.sum((1, 2))
    here = lax.dynamic_index_in_dim(t, z, 0, keepdims=False)
    own_chip = lax.dynamic_index_in_dim(here, y, 0, keepdims=False)
    other_chip = lax.dynamic_index_in_dim(here, 1 - y, 0, keepdims=False)

    def scale(log):
        return jnp.exp(log)[:, None, None]

    kv_chip = scale(own_chip[1]) * core0[0] + core1[0]
    qd_chip = core0[1] + scale(own_chip[0]) * core1[1]
    sent = jnp.where(y == 0, kv_chip, qd_chip).astype(BF16)
    neighbour = lax.ppermute(sent, "seq", swap_chip).astype(F32)
    plane = jnp.where(y == 0, qd_chip, kv_chip) + scale(own_chip.sum(0)) * neighbour
    travelling = plane.astype(BF16)
    direction = jnp.where(y == 0, 1, -1)
    beyond = jnp.zeros_like(plane)
    log = jnp.zeros((half,), F32)
    for hop in range(1, 4):
        travelling = lax.ppermute(travelling, "seq", onward)
        beyond = beyond + scale(log) * travelling.astype(F32)
        at = jnp.clip(z + direction * hop, 0, 3)
        log = log + lax.dynamic_index_in_dim(plane_totals, at, 0, keepdims=False)
    beyond = beyond.astype(BF16)
    other = lax.ppermute(beyond, "seq", swap_chip)
    before = jnp.where(y == 1, beyond, other).astype(F32)
    after = jnp.where(y == 0, beyond, other).astype(F32)
    other_scale = scale(other_chip.sum(0))
    before = jnp.where(y == 0, before, other_scale * before + neighbour)
    after = jnp.where(y == 1, after, other_scale * after + neighbour)
    for0 = jnp.stack([before, scale(own_chip[1]) * after + core1[1]])
    for1 = jnp.stack([scale(own_chip[0]) * before + core0[0], after])
    keep = jnp.where(c == 0, for0, for1).astype(BF16)
    give = jnp.where(c == 0, for1, for0).astype(BF16)
    took = lax.ppermute(give, "seq", swap_core)
    low = jnp.where(c == 0, keep, took)
    high = jnp.where(c == 0, took, keep)
    both = jnp.concatenate([low, high], axis=1)
    return both[0], both[1]


def gathered_scan(kv, qd, totals, index):
    kv_all = lax.all_gather(kv[None], "seq", axis=0, tiled=True)
    qd_all = lax.all_gather(qd[None], "seq", axis=0, tiled=True)
    before = jnp.cumsum(totals, axis=0) - totals
    after = before + totals
    own_start = lax.dynamic_index_in_dim(before, index, 0, keepdims=False)
    own_end = lax.dynamic_index_in_dim(after, index, 0, keepdims=False)
    ids = jnp.arange(totals.shape[0])[:, None]
    earlier, later = ids < index, ids > index
    pre = jnp.where(earlier, jnp.exp(jnp.where(earlier, own_start[None] - after, 0.0)), 0.0)
    post = jnp.where(later, jnp.exp(jnp.where(later, before - own_end[None], 0.0)), 0.0)
    prefix = jnp.sum(pre[:, :, None, None] * kv_all.astype(F32), axis=0)
    suffix = jnp.sum(post[:, :, None, None] * qd_all.astype(F32), axis=0)
    return prefix.astype(BF16), suffix.astype(BF16)


def plane_rows(x_rows, index):
    length, width = x_rows.shape
    place = index % 4
    parts = x_rows.reshape(length, 4, 4, width // 16)

    def columns(p):
        return lax.dynamic_index_in_dim(parts, p, 2, keepdims=False).reshape(length, width // 4)

    held = [columns(place)]
    for k in (1, 2, 3):
        held.append(lax.ppermute(columns(place ^ k), "seq", step(lambda i: i ^ k, 16)))
    return held


def laid_out(held):
    return jnp.concatenate(held, axis=0).T


def plane_values(dv):
    core = lax.ppermute(dv, "seq", step(lambda i: i ^ 1, 16))
    chip = lax.ppermute(dv, "seq", step(lambda i: i ^ 2, 16))
    both = lax.ppermute(chip, "seq", step(lambda i: i ^ 1, 16))
    return jnp.concatenate([dv, core, chip, both], axis=0)


def planes_sum(blocks, index):
    z = index // 4

    def pick(i):
        return lax.dynamic_index_in_dim(blocks, jnp.clip(i, 0, 3), 0, keepdims=False)

    up = down = None
    for s in (1, 2, 3):
        to_up, to_down = pick(4 - s + z), pick(z - 4 + s)
        if up is not None:
            to_up = (to_up.astype(F32) + up.astype(F32)).astype(BF16)
            to_down = (to_down.astype(F32) + down.astype(F32)).astype(BF16)
        up = lax.ppermute(to_up, "seq", step(lambda i: i + 4 if i // 4 < s else None, 12))
        down = lax.ppermute(
            to_down, "seq", [(15 - a, 15 - b) for a, b in step(lambda i: i + 4 if i // 4 < s else None, 12)]
        )
    return (pick(z).astype(F32) + up.astype(F32) + down.astype(F32)).astype(BF16)


def on_device(blocks, x_rows, queries, keys, values, out_grad, log_decay):
    length, heads = log_decay.shape
    size = queries.shape[1] // heads
    index = lax.axis_index("seq")
    planes = blocks == 16 and x_rows.shape[1] % 16 == 0
    cumul = jnp.cumsum(log_decay, axis=0)
    lines = cumul.T[:, None, :]
    totals = lax.all_gather(cumul[-1:], "seq", axis=0, tiled=True)
    if planes:
        x_held = plane_rows(x_rows, index)
    chunks = CHUNKS if heads % (2 * CHUNKS) == 0 else 1
    count = heads // chunks
    square, state = 2 * length * length * size, 2 * length * size * size
    call = functools.partial(per_head, length=length, size=size)

    if planes and heads % 8 == 0:
        kv, qd = call(
            states_kernel, 0, heads, kinds="wwwwl", outs=[("s", BF16)] * 2,
            flops=2 * state, args=(queries, keys, values, out_grad, lines),
        )
        kv, qd, x_held = lax.optimization_barrier((kv, qd, x_held))
        prefix, suffix = plane_scan(kv, qd, totals, index)
        return mega(
            blocks, 16 if heads % 16 == 0 else 8, laid_out(x_held), queries, keys, values, out_grad, lines, prefix, suffix
        )

    states = [
        call(
            states_kernel, i * count, count, kinds="wwwwl", outs=[("s", BF16)] * 2,
            flops=2 * state, args=(queries, keys, values, out_grad, lines),
        )
        for i in range(chunks)
    ]
    local = [
        call(
            value_local_kernel, i * count, count, kinds="wwwl", outs=[("c", F32)],
            flops=2 * square, args=(queries, keys, out_grad, lines),
        )[0]
        for i in range(chunks)
    ]
    scan = plane_scan if planes else gathered_scan
    prefixes, suffixes, value_grads, sums = [], [], [], []
    for i in range(chunks):
        own = slice(i * count, (i + 1) * count)
        prefix, suffix = scan(*states[i], totals[:, own], index)
        prefixes.append(prefix)
        suffixes.append(suffix)
        (dv,) = call(
            value_finish_kernel, i * count, count, kinds="cwls", outs=[("c", BF16)],
            flops=state, args=(local[i], keys, lines, suffix),
        )
        value_grads.append(dv)
        if planes:
            part = dot(laid_out(x_held), plane_values(dv), ((1,), (0,))).astype(BF16)
            part = part.reshape(4, part.shape[0] // 4, part.shape[1])
            sums.append(planes_sum(part, index))
        else:
            part = dot(x_rows, dv, ((0,), (0,))).astype(BF16)
            sums.append(lax.psum_scatter(part, "seq", scatter_dimension=0, tiled=True))
    query_gradient, key_grad = call(
        query_key_kernel, 0, heads, kinds="wwwwlss", outs=[("c", BF16)] * 2,
        flops=3 * square + 2 * state,
        args=(
            queries, keys, values, out_grad, lines,
            jnp.concatenate(prefixes), jnp.concatenate(suffixes),
        ),
    )
    return (
        query_gradient,
        key_grad,
        jnp.concatenate(value_grads, axis=1),
        jnp.concatenate(sums, axis=1),
    )


def solution(mesh):
    spread = P(("groups", "seq"), "heads")
    return jax.shard_map(
        functools.partial(on_device, mesh.shape["seq"]),
        mesh=mesh,
        in_specs=(P(("groups", "seq"), None),) + (spread,) * 5,
        out_specs=(spread,) * 4,
        check_vma=False,
    )
```

```python
import functools

import jax
import jax.numpy as jnp
from jax import lax
from jax.experimental import pallas as pl
from jax.experimental.pallas import tpu as pltpu
from jax.sharding import PartitionSpec as P

F32 = jnp.float32
BF16 = jnp.bfloat16
CHUNKS = 4


def dot(a, b, dims):
    return lax.dot_general(a, b, (dims, ((), ())), preferred_element_type=F32)


def columns_of(row, width):
    return jnp.broadcast_to(row, (width, row.shape[1])).T


def decay_matrix(row, width):
    length = row.shape[1]
    gap = columns_of(row, width)[:, :1] - row
    t = lax.broadcasted_iota(jnp.int32, (length, length), 0)
    s = lax.broadcasted_iota(jnp.int32, (length, length), 1)
    return jnp.where(t >= s, jnp.exp(jnp.where(t >= s, gap, 0.0)), 0.0)


def states_kernel(q_ref, k_ref, v_ref, g_ref, cum_ref, kv_ref, qd_ref):
    row = cum_ref[0]
    width = q_ref.shape[1]
    length = row.shape[1]
    cum = columns_of(row, width)
    total = row[:, length - 1 :]
    keys = (k_ref[...].astype(F32) * jnp.exp(total - cum)).astype(BF16)
    queries = (q_ref[...].astype(F32) * jnp.exp(cum)).astype(BF16)
    kv_ref[0] = dot(keys, v_ref[...], ((0,), (0,))).astype(BF16)
    qd_ref[0] = dot(queries, g_ref[...], ((0,), (0,))).astype(BF16)


def value_local_kernel(q_ref, k_ref, g_ref, cum_ref, out_ref):
    decays = decay_matrix(cum_ref[0], q_ref.shape[1])
    mixed = (dot(q_ref[...], k_ref[...], ((1,), (1,))) * decays).astype(BF16)
    out_ref[...] = dot(mixed, g_ref[...], ((0,), (0,)))


def value_finish_kernel(local_ref, k_ref, cum_ref, suffix_ref, out_ref):
    row = cum_ref[0]
    cum = columns_of(row, k_ref.shape[1])
    to_end = jnp.exp(row[:, row.shape[1] - 1 :] - cum)
    part = dot(k_ref[...], suffix_ref[0], ((1,), (0,)))
    out_ref[...] = (local_ref[...] + to_end * part).astype(BF16)


def query_key_kernel(q_ref, k_ref, v_ref, g_ref, cum_ref, prefix_ref, suffix_ref, qg_ref, kg_ref):
    row = cum_ref[0]
    width = q_ref.shape[1]
    cum = columns_of(row, width)
    to_end = jnp.exp(row[:, row.shape[1] - 1 :] - cum)
    decays = decay_matrix(row, width)
    weighted = (dot(g_ref[...], v_ref[...], ((1,), (1,))) * decays).astype(BF16)
    qg = dot(weighted, k_ref[...], ((1,), (0,)))
    qg = qg + jnp.exp(cum) * dot(g_ref[...], prefix_ref[0], ((1,), (1,)))
    kg = dot(weighted, q_ref[...], ((0,), (0,)))
    kg = kg + to_end * dot(v_ref[...], suffix_ref[0], ((1,), (1,)))
    qg_ref[...] = qg.astype(BF16)
    kg_ref[...] = kg.astype(BF16)


def per_head(body, first, count, length, size, kinds, outs, flops, args):
    specs = {
        "w": pl.BlockSpec((length, size), lambda h: (0, first + h)),
        "c": pl.BlockSpec((length, size), lambda h: (0, h)),
        "l": pl.BlockSpec((1, 1, length), lambda h: (first + h, 0, 0)),
        "s": pl.BlockSpec((1, size, size), lambda h: (h, 0, 0)),
    }
    shapes = {
        "c": (length, count * size),
        "s": (count, size, size),
    }
    moved = count * length * size * 2 * (len(kinds) + len(outs))
    return pl.pallas_call(
        body,
        grid=(count,),
        in_specs=[specs[kind] for kind in kinds],
        out_specs=[specs[kind] for kind, _ in outs],
        out_shape=[jax.ShapeDtypeStruct(shapes[kind], dtype) for kind, dtype in outs],
        cost_estimate=pl.CostEstimate(
            flops=count * flops, bytes_accessed=moved, transcendentals=count * length * length
        ),
        compiler_params=pltpu.CompilerParams(vmem_limit_bytes=32 * 1024 * 1024),
    )(*args)


def mega_kernel(
    blocks, x_ref, q_ref, k_ref, v_ref, g_ref, cum_ref, prefix_ref, suffix_ref,
    qg_ref, kg_ref, dv_ref, wg_ref,
    held, part, landed, plane_send, plane_recv, line_send, line_recv,
):
    index = lax.axis_index("seq")
    z = index // 4
    last = blocks // 4 - 1
    core, chip = index + 1 - 2 * (index % 2), index + 2 - 4 * ((index // 2) % 2)
    chunks, length, width = held.shape[0], q_ref.shape[0], held.shape[2]
    size = prefix_ref.shape[1]
    group = width // size
    rows = part.shape[2]

    barrier = pltpu.get_barrier_semaphore()

    def greet(device):
        pl.semaphore_signal(
            barrier, inc=1, device_id={"seq": device}, device_id_type=pl.DeviceIdType.MESH
        )

    greet(core)
    greet(chip)

    @pl.when(z > 0)
    def _():
        greet(index - 4)

    @pl.when(z < last)
    def _():
        greet(index + 4)

    inner = (z > 0) & (z < last)
    pl.when(inner)(lambda: pl.semaphore_wait(barrier, 4))
    pl.when(jnp.logical_not(inner))(lambda: pl.semaphore_wait(barrier, 3))

    def plane_copy(j, source, target, device):
        return pltpu.make_async_remote_copy(
            src_ref=held.at[j, pl.ds(source * length, length)],
            dst_ref=held.at[j, pl.ds(target * length, length)],
            send_sem=plane_send.at[target - 1, j],
            recv_sem=plane_recv.at[target - 1, j],
            device_id={"seq": device},
            device_id_type=pl.DeviceIdType.MESH,
        )

    def to_core(j):
        return plane_copy(j, 0, 1, core)

    def to_chip(j):
        return plane_copy(j, 0, 2, chip)

    def onward(j):
        return plane_copy(j, 2, 3, core)

    def line_copy(j, way, t):
        slot = t - 1 + way
        return pltpu.make_async_remote_copy(
            src_ref=part.at[j, t],
            dst_ref=landed.at[way, slot, j],
            send_sem=line_send.at[way, slot, j],
            recv_sem=line_recv.at[way, slot, j],
            device_id={"seq": index + 4 - 8 * way},
            device_id_type=pl.DeviceIdType.MESH,
        )

    def columns(j, h):
        return pl.ds(pl.multiple_of(j * width + h * size, size), size)

    def value_part(j):
        for h in range(group):
            at = columns(j, h)
            row = cum_ref[j * group + h]
            cum = columns_of(row, size)
            to_end = jnp.exp(row[:, length - 1 :] - cum)
            keys, grads = k_ref[:, at], g_ref[:, at]
            mixed = (dot(q_ref[:, at], keys, ((1,), (1,))) * decay_matrix(row, size)).astype(BF16)
            dv = dot(mixed, grads, ((0,), (0,)))
            dv = dv + to_end * dot(keys, suffix_ref[j * group + h], ((1,), (0,)))
            dv = dv.astype(BF16)
            dv_ref[:, at] = dv
            held[j, pl.ds(0, length), h * size : (h + 1) * size] = dv

    def query_key_part(j):
        for h in range(group):
            at = columns(j, h)
            row = cum_ref[j * group + h]
            cum = columns_of(row, size)
            to_end = jnp.exp(row[:, length - 1 :] - cum)
            keys, grads, values, queries = k_ref[:, at], g_ref[:, at], v_ref[:, at], q_ref[:, at]
            weighted = dot(grads, values, ((1,), (1,))) * decay_matrix(row, size)
            weighted = weighted.astype(BF16)
            qg = dot(weighted, keys, ((1,), (0,)))
            qg = qg + jnp.exp(cum) * dot(grads, prefix_ref[j * group + h], ((1,), (1,)))
            kg = dot(weighted, queries, ((0,), (0,)))
            kg = kg + to_end * dot(values, suffix_ref[j * group + h], ((1,), (1,)))
            qg_ref[:, at] = qg.astype(BF16)
            kg_ref[:, at] = kg.astype(BF16)

    def within(j):
        return (j >= 0) & (j < chunks)

    def line_part(j, way, t):
        has_source = z > 0 if way == 0 else z < last
        ahead = t > z if way == 0 else t < z

        @pl.when(has_source)
        def _():
            line_copy(j, way, t).wait_recv()
            slot = t - 1 + way
            part[j, t] = (part[j, t].astype(F32) + landed[way, slot, j].astype(F32)).astype(BF16)

        @pl.when(ahead)
        def _():
            line_copy(j, way, t).start()

    def line_stage(j, way):
        order = range(last, 0, -1) if way == 0 else range(last)
        for t in order:
            reached = z <= t if way == 0 else z >= t
            pl.when(within(j) & reached)(functools.partial(line_part, j, way, t))

    @pl.loop(0, chunks + 2 + last)
    def _(i):
        @pl.when(i < chunks)
        def _():
            value_part(i)
            to_chip(i).start()
            to_core(i).start()

        @pl.when(within(i - 1))
        def _():
            to_chip(i - 1).wait_recv()
            onward(i - 1).start()

        j = i - 2

        @pl.when(within(j))
        def _():
            to_core(j).wait_recv()
            onward(j).wait_recv()
            for t in range(last + 1):
                part[j, t] = dot(
                    x_ref[t * rows : (t + 1) * rows, :], held[j], ((1,), (0,))
                ).astype(BF16)

        line_stage(j - z, 0)
        line_stage(j - last + z, 1)

        @pl.when(within(j))
        def _():
            query_key_part(j)

        done = j - last

        @pl.when(within(done))
        def _():
            at = pl.ds(pl.multiple_of(done * width, width), width)
            wg_ref[:, at] = part[done, z]

    @pl.loop(0, chunks)
    def _(j):
        to_core(j).wait_send()
        to_chip(j).wait_send()
        onward(j).wait_send()
        for t in range(last + 1):
            if t > 0:
                pl.when(t > z)(lambda t=t: line_copy(j, 0, t).wait_send())
            if t < last:
                pl.when(t < z)(lambda t=t: line_copy(j, 1, t).wait_send())


def mega(blocks, chunks, x_held, queries, keys, values, out_grad, lines, prefix, suffix):
    length, columns = queries.shape
    width, planes = columns // chunks, blocks // 4
    rows = x_held.shape[0] // planes
    heads, size = prefix.shape[0], prefix.shape[1]
    vmem = pl.BlockSpec(memory_space=pltpu.VMEM)
    whole = jax.ShapeDtypeStruct((length, columns), BF16)
    dma = pltpu.SemaphoreType.DMA
    return pl.pallas_call(
        functools.partial(mega_kernel, blocks),
        out_shape=[whole, whole, whole, jax.ShapeDtypeStruct((rows, columns), BF16)],
        in_specs=[vmem] * 8,
        out_specs=[vmem] * 4,
        scratch_shapes=[
            pltpu.VMEM((chunks, 4 * length, width), BF16),
            pltpu.VMEM((chunks, planes, rows, width), BF16),
            pltpu.VMEM((2, planes - 1, chunks, rows, width), BF16),
            dma((3, chunks)),
            dma((3, chunks)),
            dma((2, planes - 1, chunks)),
            dma((2, planes - 1, chunks)),
        ],
        cost_estimate=pl.CostEstimate(
            flops=heads * (10 * length * length * size + 8 * length * size * size)
            + 2 * x_held.size * columns * 4,
            bytes_accessed=16 * length * columns,
            transcendentals=2 * heads * length * length,
        ),
        compiler_params=pltpu.CompilerParams(
            collective_id=0, has_side_effects=True, vmem_limit_bytes=60 * 1024 * 1024
        ),
    )(x_held, queries, keys, values, out_grad, lines, prefix, suffix)


def step(mapping, count):
    return [(i, mapping(i)) for i in range(count) if mapping(i) is not None]


def plane_scan(kv, qd, totals, index):
    heads = kv.shape[0]
    half = heads // 2
    z, y, c = index // 4, (index // 2) % 2, index % 2
    swap_core = step(lambda i: i ^ 1, 16)
    swap_chip = step(lambda i: i ^ 2, 16)
    onward = step(
        lambda i: (i + 4 if i + 4 < 16 else None) if i & 2 else (i - 4 if i >= 4 else None), 16
    )

    def mine(a, which):
        return lax.dynamic_slice_in_dim(a, which * half, half, axis=-3)

    stack = jnp.stack([kv, qd])
    got = lax.ppermute(mine(stack, 1 - c), "seq", swap_core)
    own = mine(stack, c)
    core0 = jnp.where(c == 0, own, got).astype(F32)
    core1 = jnp.where(c == 0, got, own).astype(F32)
    t = lax.dynamic_slice_in_dim(totals, c * half, half, axis=1).reshape(4, 2, 2, half)
    plane_totals = t.sum((1, 2))
    here = lax.dynamic_index_in_dim(t, z, 0, keepdims=False)
    own_chip = lax.dynamic_index_in_dim(here, y, 0, keepdims=False)
    other_chip = lax.dynamic_index_in_dim(here, 1 - y, 0, keepdims=False)

    def scale(log):
        return jnp.exp(log)[:, None, None]

    kv_chip = scale(own_chip[1]) * core0[0] + core1[0]
    qd_chip = core0[1] + scale(own_chip[0]) * core1[1]
    sent = jnp.where(y == 0, kv_chip, qd_chip).astype(BF16)
    neighbour = lax.ppermute(sent, "seq", swap_chip).astype(F32)
    plane = jnp.where(y == 0, qd_chip, kv_chip) + scale(own_chip.sum(0)) * neighbour
    travelling = plane.astype(BF16)
    direction = jnp.where(y == 0, 1, -1)
    beyond = jnp.zeros_like(plane)
    log = jnp.zeros((half,), F32)
    for hop in range(1, 4):
        travelling = lax.ppermute(travelling, "seq", onward)
        beyond = beyond + scale(log) * travelling.astype(F32)
        at = jnp.clip(z + direction * hop, 0, 3)
        log = log + lax.dynamic_index_in_dim(plane_totals, at, 0, keepdims=False)
    beyond = beyond.astype(BF16)
    other = lax.ppermute(beyond, "seq", swap_chip)
    before = jnp.where(y == 1, beyond, other).astype(F32)
    after = jnp.where(y == 0, beyond, other).astype(F32)
    other_scale = scale(other_chip.sum(0))
    before = jnp.where(y == 0, before, other_scale * before + neighbour)
    after = jnp.where(y == 1, after, other_scale * after + neighbour)
    for0 = jnp.stack([before, scale(own_chip[1]) * after + core1[1]])
    for1 = jnp.stack([scale(own_chip[0]) * before + core0[0], after])
    keep = jnp.where(c == 0, for0, for1).astype(BF16)
    give = jnp.where(c == 0, for1, for0).astype(BF16)
    took = lax.ppermute(give, "seq", swap_core)
    low = jnp.where(c == 0, keep, took)
    high = jnp.where(c == 0, took, keep)
    both = jnp.concatenate([low, high], axis=1)
    return both[0], both[1]


def gathered_scan(kv, qd, totals, index):
    kv_all = lax.all_gather(kv[None], "seq", axis=0, tiled=True)
    qd_all = lax.all_gather(qd[None], "seq", axis=0, tiled=True)
    before = jnp.cumsum(totals, axis=0) - totals
    after = before + totals
    own_start = lax.dynamic_index_in_dim(before, index, 0, keepdims=False)
    own_end = lax.dynamic_index_in_dim(after, index, 0, keepdims=False)
    ids = jnp.arange(totals.shape[0])[:, None]
    earlier, later = ids < index, ids > index
    pre = jnp.where(earlier, jnp.exp(jnp.where(earlier, own_start[None] - after, 0.0)), 0.0)
    post = jnp.where(later, jnp.exp(jnp.where(later, before - own_end[None], 0.0)), 0.0)
    prefix = jnp.sum(pre[:, :, None, None] * kv_all.astype(F32), axis=0)
    suffix = jnp.sum(post[:, :, None, None] * qd_all.astype(F32), axis=0)
    return prefix.astype(BF16), suffix.astype(BF16)


def plane_rows(x_rows, index):
    length, width = x_rows.shape
    place = index % 4
    parts = x_rows.reshape(length, 4, 4, width // 16)

    def columns(p):
        return lax.dynamic_index_in_dim(parts, p, 2, keepdims=False).reshape(length, width // 4)

    held = [columns(place)]
    for k in (1, 2, 3):
        held.append(lax.ppermute(columns(place ^ k), "seq", step(lambda i: i ^ k, 16)))
    return held


def laid_out(held):
    return jnp.concatenate(held, axis=0).T


def plane_values(dv):
    core = lax.ppermute(dv, "seq", step(lambda i: i ^ 1, 16))
    chip = lax.ppermute(dv, "seq", step(lambda i: i ^ 2, 16))
    both = lax.ppermute(chip, "seq", step(lambda i: i ^ 1, 16))
    return jnp.concatenate([dv, core, chip, both], axis=0)


def planes_sum(blocks, index):
    z = index // 4

    def pick(i):
        return lax.dynamic_index_in_dim(blocks, jnp.clip(i, 0, 3), 0, keepdims=False)

    up = down = None
    for s in (1, 2, 3):
        to_up, to_down = pick(4 - s + z), pick(z - 4 + s)
        if up is not None:
            to_up = (to_up.astype(F32) + up.astype(F32)).astype(BF16)
            to_down = (to_down.astype(F32) + down.astype(F32)).astype(BF16)
        up = lax.ppermute(to_up, "seq", step(lambda i: i + 4 if i // 4 < s else None, 12))
        down = lax.ppermute(
            to_down, "seq", [(15 - a, 15 - b) for a, b in step(lambda i: i + 4 if i // 4 < s else None, 12)]
        )
    return (pick(z).astype(F32) + up.astype(F32) + down.astype(F32)).astype(BF16)


def on_device(blocks, x_rows, queries, keys, values, out_grad, log_decay):
    length, heads = log_decay.shape
    size = queries.shape[1] // heads
    index = lax.axis_index("seq")
    planes = blocks == 16 and x_rows.shape[1] % 16 == 0
    cumul = jnp.cumsum(log_decay, axis=0)
    lines = cumul.T[:, None, :]
    totals = lax.all_gather(cumul[-1:], "seq", axis=0, tiled=True)
    if planes:
        x_held = plane_rows(x_rows, index)
    chunks = CHUNKS if heads % (2 * CHUNKS) == 0 else 1
    count = heads // chunks
    square, state = 2 * length * length * size, 2 * length * size * size
    call = functools.partial(per_head, length=length, size=size)

    if planes and heads % 8 == 0:
        kv, qd = call(
            states_kernel, 0, heads, kinds="wwwwl", outs=[("s", BF16)] * 2,
            flops=2 * state, args=(queries, keys, values, out_grad, lines),
        )
        kv, qd, x_held = lax.optimization_barrier((kv, qd, x_held))
        cut = heads // 2
        scans = [
            plane_scan(kv[own], qd[own], totals[:, own], index)
            for own in (slice(0, cut), slice(cut, heads))
        ]
        prefix, suffix = (jnp.concatenate(halves) for halves in zip(*scans))
        return mega(
            blocks, 16 if heads % 16 == 0 else 8, laid_out(x_held), queries, keys, values, out_grad, lines, prefix, suffix
        )

    states = [
        call(
            states_kernel, i * count, count, kinds="wwwwl", outs=[("s", BF16)] * 2,
            flops=2 * state, args=(queries, keys, values, out_grad, lines),
        )
        for i in range(chunks)
    ]
    local = [
        call(
            value_local_kernel, i * count, count, kinds="wwwl", outs=[("c", F32)],
            flops=2 * square, args=(queries, keys, out_grad, lines),
        )[0]
        for i in range(chunks)
    ]
    scan = plane_scan if planes else gathered_scan
    prefixes, suffixes, value_grads, sums = [], [], [], []
    for i in range(chunks):
        own = slice(i * count, (i + 1) * count)
        prefix, suffix = scan(*states[i], totals[:, own], index)
        prefixes.append(prefix)
        suffixes.append(suffix)
        (dv,) = call(
            value_finish_kernel, i * count, count, kinds="cwls", outs=[("c", BF16)],
            flops=state, args=(local[i], keys, lines, suffix),
        )
        value_grads.append(dv)
        if planes:
            part = dot(laid_out(x_held), plane_values(dv), ((1,), (0,))).astype(BF16)
            part = part.reshape(4, part.shape[0] // 4, part.shape[1])
            sums.append(planes_sum(part, index))
        else:
            part = dot(x_rows, dv, ((0,), (0,))).astype(BF16)
            sums.append(lax.psum_scatter(part, "seq", scatter_dimension=0, tiled=True))
    query_gradient, key_grad = call(
        query_key_kernel, 0, heads, kinds="wwwwlss", outs=[("c", BF16)] * 2,
        flops=3 * square + 2 * state,
        args=(
            queries, keys, values, out_grad, lines,
            jnp.concatenate(prefixes), jnp.concatenate(suffixes),
        ),
    )
    return (
        query_gradient,
        key_grad,
        jnp.concatenate(value_grads, axis=1),
        jnp.concatenate(sums, axis=1),
    )


def solution(mesh):
    spread = P(("groups", "seq"), "heads")
    return jax.shard_map(
        functools.partial(on_device, mesh.shape["seq"]),
        mesh=mesh,
        in_specs=(P(("groups", "seq"), None),) + (spread,) * 5,
        out_specs=(spread,) * 4,
        check_vma=False,
    )
```
